256 devices in a mesh: pipe: 8 (over z_hi, core), expert: 32 (over y, z_lo, x).
Axes of the slice: x: 4, y: 4, z: 8 (z_hi: 4, z_lo: 2; z = z_hi * 2 + z_lo), core: 2. Of those that a mesh axis runs over, the one named last changes fastest.
Arguments:
- tokens_fwd: bfloat16 [32768, 3584], P(('pipe', 'expert')), may hold values from -6 to 6
- route_fwd: int32 [32768, 1], P(('pipe', 'expert')), may hold values from 0 to 7; in each aligned block of 128 rows (0 to 127, 128 to 255, ...) at most 24 rows name the same one
- gate_fwd: float32 [32768, 1], P(('pipe', 'expert')), may hold values from 0.2 to 2
- grad_out: bfloat16 [32768, 3584], P(('pipe', 'expert')), may hold values from -6 to 6
- route_bwd: int32 [32768, 1], P(('pipe', 'expert')), may hold values from 0 to 7; in each aligned block of 128 rows (0 to 127, 128 to 255, ...) at most 24 rows name the same one
- gate_bwd: float32 [32768, 1], P(('pipe', 'expert')), may hold values from 0.2 to 2
- saved_pre: bfloat16 [8, 768, 2, 8192], P('pipe', None, None, 'expert'), may hold values from -6 to 6
- w_in: bfloat16 [8, 3584, 2, 8192], P('pipe', None, None, 'expert'), may hold values from -0.09375 to 0.09375
- w_down: bfloat16 [8, 8192, 3584], P('pipe', 'expert'), may hold values from -0.1875 to 0.1875
- att_grad: float32 [8, 3584, 1536], P('pipe', 'expert'), may hold values from -6 to 6
Outputs:
- mixed_fwd: bfloat16 [32768, 3584], P(('pipe', 'expert'))
- grad_in: bfloat16 [32768, 3584], P(('pipe', 'expert'))
- att_sum: float32 [8, 3584, 1536], P('pipe', 'expert')
The draws below stay inside these ranges and needn't reach their ends.
Inputs may be any that keep to these rules, and one draw needn't show every extreme that they name: `route_fwd`: each row names one of the 8 experts; among the 128 rows of one device no expert is named more than 24 times, and that count is reached on some device. `route_bwd`: as for route_fwd, drawn independently.
All inputs are finite; a program needn't handle non-finite values.
Results may differ from the reference program's by a relative error of at most 0.012.
Values may be sent and summed in bfloat16 or wider, within the bound.
No kernel may reach another device: no remote copies, remote signals or barrier semaphores. Data moves between devices by JAX's collectives and lax.ppermute only.
A program may use at most 128 MiB of HBM per device.

```python
import math
import jax
import jax.numpy as jnp
import numpy as np
from jax import lax

DM = 3584
FH = 1024
QRANK = 1536
ESPLIT = 4
TOP = 1
TOK = 128
EXPERTS = 8
CAP = 24
TOKENS = 32768
N_PIPE = 8
N_EXPERT = 32


def levels(stream_key, extent, split, least, top_value):
    factor_of = 1.0
    for axis_at, shards_of in split:
        steps = jax.random.uniform(jax.random.fold_in(jax.random.fold_in(stream_key, 6), axis_at), (shards_of,), jnp.float32, least / len(split), top_value / len(split))
        factor_of = factor_of * jnp.repeat(jnp.exp(steps), extent[axis_at] // shards_of).reshape((-1,) + (1,) * (len(extent) - 1 - axis_at))
    return factor_of


def routed_block(key, own, number, rows, amount, top, most, skew):
    ranking = jax.random.permutation(key, amount)
    crowded, ordinary = load_shares(amount, rows * top, most, skew, True), load_shares(amount, rows * top, most, skew, False)
    places = jnp.arange(amount)

    def named(tallies, turn):
        used = int((tallies > 0).sum())
        fixed = max(1, used // 4)
        shifted = fixed + (places - fixed + turn * (used - fixed)) % max(1, amount - fixed)
        return jnp.zeros((amount,), jnp.int32).at[ranking[jnp.where(places < fixed, places, shifted)]].set(jnp.asarray(tallies, jnp.int32))

    tallies = jnp.where(number % 4 == 0, named(crowded, number // 4), named(ordinary, number - number // 4 - 1))
    mixed = jax.random.permutation(jax.random.fold_in(own, 3), amount)
    source_of, sink = mixed[0:amount // 2 * 2:2], mixed[1:amount // 2 * 2:2]
    room = jnp.minimum(tallies[source_of] - 1, most - tallies[sink]) // 2
    room = jnp.where((source_of == ranking[0]) | (sink == ranking[0]) | (tallies[sink] == 0), 0, jnp.maximum(room, 0))
    shifted = jax.random.randint(jax.random.fold_in(own, 4), (amount // 2,), 0, 1 << 20) % (room + 1)
    tallies = tallies.at[source_of].add(-shifted).at[sink].add(shifted)
    labels = jnp.searchsorted(jnp.cumsum(tallies), jnp.arange(rows * top), side="right").astype(jnp.int32)
    table = labels.reshape(top, rows).T
    table = table[jax.random.permutation(jax.random.fold_in(own, 1), rows)]
    turn = jax.random.randint(jax.random.fold_in(own, 2), (rows, 1), 0, top)
    return jnp.take_along_axis(table, (jnp.arange(top)[None, :] + turn) % top, axis=1)


def load_shares(amount, total, most, slope, full):
    portions = [(1 << 20) // math.isqrt(standing ** slope) + 1 for standing in range(1, amount + 1)]
    largest = most if full else min(most, max(-(-total // amount), total * portions[0] // sum(portions)))
    least = 1 if total - largest >= amount - 1 else 0
    counts, spare = [largest] + [least] * (amount - 1), total - largest - least * (amount - 1)
    while spare > 0:
        movable = [i for i in range(1, amount) if counts[i] < largest] or [i for i in range(1, amount) if counts[i] < most]
        whole, remaining = sum([portions[i] for i in movable]), spare
        for i in movable:
            extra = min(most - counts[i], max(1, remaining * portions[i] // whole), spare)
            counts[i] = counts[i] + extra
            spare = spare - extra
    return np.array(counts)


def normal_values(rng, extent, deviation, limit, pieces=(), kind=jnp.bfloat16):
    values = deviation * jax.random.normal(rng, extent, jnp.float32)
    if pieces:
        values = values * levels(rng, extent, pieces, -0.22, 0.18)
    return jnp.clip(values, -limit, limit).astype(kind)


def setup_inputs(seed: int = 0) -> dict:
    keys = jax.random.split(jax.random.key(seed), 11)
    tokens_fwd = normal_values(keys[0], (TOKENS, DM), 1.0, 6.0, ((0, 256),))
    route_fwd_keys = jax.random.split(jax.random.fold_in(keys[1], 1), TOKENS // TOK)
    route_fwd_turns = jax.random.permutation(jax.random.fold_in(keys[1], 3), TOKENS // TOK)
    route_fwd = jax.vmap(lambda own, number: routed_block(jax.random.fold_in(keys[1], 2), own, number, TOK, EXPERTS, TOP, CAP, 2))(route_fwd_keys, route_fwd_turns).reshape((TOKENS, TOP))
    gate_fwd = jnp.clip(jnp.exp(math.log(2.0) - 2.3025851 * jax.random.uniform(keys[2], (TOKENS, TOP), jnp.float32) ** levels(keys[2], (TOKENS, TOP), ((0, 256),), -0.2, 0.2)), 0.2, 2.0)
    grad_out = normal_values(keys[3], (TOKENS, DM), 1.0, 6.0, ((0, 256),))
    route_bwd_keys = jax.random.split(jax.random.fold_in(keys[4], 1), TOKENS // TOK)
    route_bwd_turns = jax.random.permutation(jax.random.fold_in(keys[4], 3), TOKENS // TOK)
    route_bwd = jax.vmap(lambda own, number: routed_block(jax.random.fold_in(keys[4], 2), own, number, TOK, EXPERTS, TOP, CAP, 2))(route_bwd_keys, route_bwd_turns).reshape((TOKENS, TOP))
    gate_bwd = jnp.clip(jnp.exp(math.log(2.0) - 2.3025851 * jax.random.uniform(keys[5], (TOKENS, TOP), jnp.float32) ** levels(keys[5], (TOKENS, TOP), ((0, 256),), -0.2, 0.2)), 0.2, 2.0)
    saved_pre = normal_values(keys[6], (N_PIPE, N_EXPERT * CAP, 2, EXPERTS * FH), 1.0, 6.0, ((0, 8), (3, 32)))
    w_in = normal_values(keys[7], (N_PIPE, DM, 2, EXPERTS * FH), DM ** -0.5, 0.09375, ((0, 8), (3, 32)))
    w_down = normal_values(keys[8], (N_PIPE, EXPERTS * FH, DM), FH ** -0.5, 0.1875, ((0, 8), (1, 32)))
    att_grad = normal_values(keys[9], (N_PIPE, DM, QRANK), 1.0, 6.0, ((0, 8), (1, 32)), jnp.float32)
    return dict(tokens_fwd=tokens_fwd, route_fwd=route_fwd, gate_fwd=gate_fwd, grad_out=grad_out, route_bwd=route_bwd, gate_bwd=gate_bwd, saved_pre=saved_pre, w_in=w_in, w_down=w_down, att_grad=att_grad)


def slot_positions(route):
    hits = (route[:, None] == jnp.arange(EXPERTS, dtype=jnp.int32)[None, :]).astype(jnp.int32)
    hits = hits.reshape(N_EXPERT, TOK, EXPERTS)
    before = jnp.cumsum(hits, axis=1) - hits
    slot = jnp.sum(before * hits, axis=2).reshape(-1)
    source = jnp.arange(N_EXPERT * TOK, dtype=jnp.int32) // TOK
    return (source * CAP + slot).astype(jnp.int32)


def expert_pass(tok_rows, route, gate, work):
    slots_all = N_EXPERT * CAP
    positions = slot_positions(route)

    def step(accum, expert_id):
        routed = route == expert_id
        target = jnp.where(routed, positions, slots_all)
        buffer = jnp.zeros((slots_all, DM), jnp.bfloat16).at[target].set(tok_rows, mode="drop")
        combined = work(buffer, expert_id)
        picked = combined[jnp.minimum(target, slots_all - 1)]
        return accum + jnp.where(routed[:, None], picked, jnp.float32(0.0)), None

    accum, _ = lax.scan(step, jnp.zeros((N_EXPERT * TOK, DM), jnp.float32), jnp.arange(EXPERTS, dtype=jnp.int32))
    return (accum * gate).astype(jnp.bfloat16)


def reference(tokens_fwd, route_fwd, gate_fwd, grad_out, route_bwd, gate_bwd, saved_pre, w_in, w_down, att_grad):
    quarter = FH // ESPLIT

    def one_rank(packed):
        tok_rows, route_a, gate_a, cotangent, route_b, gate_b, saved, w_both, w_out = packed

        def forward(buffer, expert_id):
            w_part = lax.dynamic_slice_in_dim(w_both, expert_id * FH, FH, 2)
            d_part = lax.dynamic_slice_in_dim(w_out, expert_id * FH, FH, 0)
            gate_pre = jnp.dot(buffer, w_part[:, 0, :], preferred_element_type=jnp.float32)
            up_pre = jnp.dot(buffer, w_part[:, 1, :], preferred_element_type=jnp.float32)
            hidden = (jax.nn.silu(gate_pre) * up_pre).astype(jnp.bfloat16)
            accum = jnp.zeros((buffer.shape[0], DM), jnp.float32)
            for member in range(ESPLIT):
                lower = member * quarter
                partial_value = jnp.dot(hidden[:, lower:lower + quarter], d_part[lower:lower + quarter], preferred_element_type=jnp.float32).astype(jnp.bfloat16)
                accum = accum + lax.optimization_barrier(partial_value).astype(jnp.float32)
            return accum

        def backward(buffer, expert_id):
            w_part = lax.dynamic_slice_in_dim(w_both, expert_id * FH, FH, 2)
            d_part = lax.dynamic_slice_in_dim(w_out, expert_id * FH, FH, 0)
            s_part = lax.dynamic_slice_in_dim(saved, expert_id * FH, FH, 2)
            gate_pre = s_part[:, 0, :].astype(jnp.float32)
            up_pre = s_part[:, 1, :].astype(jnp.float32)
            d_hidden = jnp.dot(buffer, d_part.T, preferred_element_type=jnp.float32)
            sig_gate = jax.nn.sigmoid(gate_pre)
            d_gate = (d_hidden * up_pre * sig_gate * (1.0 + gate_pre * (1.0 - sig_gate))).astype(jnp.bfloat16)
            d_up = (d_hidden * gate_pre * sig_gate).astype(jnp.bfloat16)
            accum = jnp.zeros((buffer.shape[0], DM), jnp.float32)
            for member in range(ESPLIT):
                lower = member * quarter
                upper = lower + quarter
                partial_value = (jnp.dot(d_gate[:, lower:upper], w_part[:, 0, lower:upper].T, preferred_element_type=jnp.float32)
                           + jnp.dot(d_up[:, lower:upper], w_part[:, 1, lower:upper].T, preferred_element_type=jnp.float32)).astype(jnp.bfloat16)
                accum = accum + lax.optimization_barrier(partial_value).astype(jnp.float32)
            return accum

        mixed = expert_pass(tok_rows, route_a[:, 0], gate_a, forward)
        grads = expert_pass(cotangent, route_b[:, 0], gate_b, backward)
        return mixed, grads

    per_rank = (tokens_fwd.reshape(N_PIPE, N_EXPERT * TOK, DM), route_fwd.reshape(N_PIPE, N_EXPERT * TOK, TOP),
                gate_fwd.reshape(N_PIPE, N_EXPERT * TOK, TOP), grad_out.reshape(N_PIPE, N_EXPERT * TOK, DM),
                route_bwd.reshape(N_PIPE, N_EXPERT * TOK, TOP), gate_bwd.reshape(N_PIPE, N_EXPERT * TOK, TOP),
                saved_pre, w_in, w_down)
    mixed, grads = lax.map(one_rank, per_rank)
    att_sum = att_grad + att_grad[::-1]
    return mixed.reshape(TOKENS, DM), grads.reshape(TOKENS, DM), att_sum
```

```python
import functools

import jax
import jax.numpy as jnp
from jax import lax
from jax.experimental import pallas as pl
from jax.experimental.pallas import tpu as pltpu
from jax.sharding import PartitionSpec as P

ESPLIT = 4
STEPS = 4
FIRST, LATER = 0.01, 0.01
BESIDE = 300
VMEM = 24 * 1024 * 1024
BOTH = ("pipe", "expert")


def pair_routes(pipes, owners):
    weights, tokens = [], []
    for p in range(pipes):
        for e in range(owners):
            x = e % ESPLIT
            near, far = e - x + (x ^ 1), e - x + (ESPLIT - 1 - x)
            here = p * owners + e
            weights.append((here, p * owners + (near if p % 2 == 0 else far)))
            tokens.append((here, p * owners + (far if p % 2 == 0 else near)))
    return weights, tokens


def weigh(work):
    return pl.CostEstimate(flops=int(work), bytes_accessed=int(work) // 128, transcendentals=0)


def dispatch_body(capacity, route_ref, rows_ref, buffer_ref, select_ref):
    route = route_ref[...]
    count = route.shape[1]
    slots = select_ref.shape[0]
    experts = lax.broadcasted_iota(jnp.int32, (8, count), 0)
    hits = jnp.concatenate(
        [(route == experts + 8 * k).astype(jnp.float32) for k in range(-(-slots // capacity // 8))]
    )
    earlier = lax.broadcasted_iota(jnp.int32, (count, count), 0) < lax.broadcasted_iota(
        jnp.int32, (count, count), 1
    )
    before = jnp.dot(
        hits.astype(jnp.bfloat16), earlier.astype(jnp.bfloat16), preferred_element_type=jnp.float32
    )
    slot = jnp.sum(before * hits, axis=0, keepdims=True).astype(jnp.int32)
    position = route * capacity + slot
    chosen = lax.broadcasted_iota(jnp.int32, (slots, count), 0) == position
    select = chosen.astype(jnp.float32).astype(jnp.bfloat16)
    select_ref[...] = select
    wide = rows_ref.shape[1] // 4
    for k in range(4):
        cols = slice(k * wide, (k + 1) * wide)
        buffer_ref[:, cols] = jnp.dot(
            select, rows_ref[:, cols], preferred_element_type=jnp.float32
        ).astype(jnp.bfloat16)


def dispatch(route, tokens, experts, capacity, scale):
    count, features = tokens.shape
    slots = experts * capacity
    return pl.pallas_call(
        functools.partial(dispatch_body, capacity),
        out_shape=(
            jax.ShapeDtypeStruct((slots, features), jnp.bfloat16),
            jax.ShapeDtypeStruct((slots, count), jnp.bfloat16),
        ),
        compiler_params=pltpu.CompilerParams(vmem_limit_bytes=VMEM),
        cost_estimate=weigh(scale * slots * count * features),
    )(route.reshape(1, count), tokens)


def dot(a, b):
    return jnp.dot(a, b, preferred_element_type=jnp.float32)


def dot_t(a, b):
    return lax.dot_general(a, b, (((1,), (1,)), ((), ())), preferred_element_type=jnp.float32)


def grad_of(d_hidden, gate_pre, up_pre):
    gate_pre, up_pre = gate_pre.astype(jnp.float32), up_pre.astype(jnp.float32)
    sig_gate = jax.nn.sigmoid(gate_pre)
    d_gate = d_hidden * up_pre * sig_gate * (1.0 + gate_pre * (1.0 - sig_gate))
    d_up = d_hidden * gate_pre * sig_gate
    return d_gate.astype(jnp.bfloat16), d_up.astype(jnp.bfloat16)


def backward_first_body(steps, rows_ref, own_ref, other_ref, stored_own, stored_other, out_ref, total):
    step = pl.program_id(0)

    @pl.when(step == 0)
    def _():
        total[...] = jnp.zeros_like(total)

    quarter = own_ref.shape[0]
    rows = rows_ref[...]
    total[:, :quarter] += dot_t(rows, own_ref[...])
    total[:, quarter:] += dot_t(rows, other_ref[...])

    @pl.when(step == steps - 1)
    def _():
        for k, stored in enumerate((stored_own, stored_other)):
            d_hidden = total[:, k * quarter : (k + 1) * quarter]
            d_gate, d_up = grad_of(d_hidden, stored[0], stored[1])
            out_ref[:, 2 * k * quarter : (2 * k + 1) * quarter] = d_gate
            out_ref[:, (2 * k + 1) * quarter : 2 * (k + 1) * quarter] = d_up


def backward_first(rows, own, other, stored_own, stored_other):
    count, features = rows.shape
    quarter, wide = own.shape[0], features // STEPS
    whole = pl.BlockSpec(stored_own.shape, lambda i: (0, 0, 0))
    return pl.pallas_call(
        functools.partial(backward_first_body, STEPS),
        grid=(STEPS,),
        in_specs=[
            pl.BlockSpec((count, wide), lambda i: (0, i)),
            pl.BlockSpec((quarter, wide), lambda i: (0, i)),
            pl.BlockSpec((quarter, wide), lambda i: (0, i)),
            whole,
            whole,
        ],
        out_specs=pl.BlockSpec((count, 4 * quarter), lambda i: (0, 0)),
        out_shape=jax.ShapeDtypeStruct((count, 4 * quarter), jnp.bfloat16),
        scratch_shapes=[pltpu.VMEM((count, 2 * quarter), jnp.float32)],
        compiler_params=pltpu.CompilerParams(vmem_limit_bytes=VMEM),
        cost_estimate=weigh(LATER * count * features * quarter),
    )(rows, own, other, stored_own, stored_other)


def backward_second_body(d_ref, own_ref, other_ref, out_ref):
    half = own_ref.shape[1]
    value = dot_t(d_ref[:, :half], own_ref[...]) + dot_t(d_ref[:, half:], other_ref[...])
    out_ref[...] = value.astype(jnp.bfloat16)


def backward_second(d_pre, own, other):
    count, (features, half) = d_pre.shape[0], own.shape
    wide = features // STEPS
    weight = pl.BlockSpec((wide, half), lambda i: (i, 0))
    return pl.pallas_call(
        backward_second_body,
        grid=(STEPS,),
        in_specs=[pl.BlockSpec(d_pre.shape, lambda i: (0, 0)), weight, weight],
        out_specs=pl.BlockSpec((count, wide), lambda i: (0, i)),
        out_shape=jax.ShapeDtypeStruct((count, features), jnp.bfloat16),
        compiler_params=pltpu.CompilerParams(vmem_limit_bytes=VMEM),
        cost_estimate=weigh(LATER * count * features * half),
    )(d_pre, own, other)


def forward_first_body(steps, rows_ref, own_ref, other_ref, out_ref, total):
    step = pl.program_id(0)

    @pl.when(step == 0)
    def _():
        total[...] = jnp.zeros_like(total)

    half = own_ref.shape[1]
    rows = rows_ref[...]
    total[:, :half] += dot(rows, own_ref[...])
    total[:, half:] += dot(rows, other_ref[...])

    @pl.when(step == steps - 1)
    def _():
        quarter = half // 2
        for k in range(2):
            gate_pre = total[:, k * half : k * half + quarter]
            up_pre = total[:, k * half + quarter : (k + 1) * half]
            hidden = jax.nn.silu(gate_pre) * up_pre
            out_ref[:, k * quarter : (k + 1) * quarter] = hidden.astype(jnp.bfloat16)


def forward_first(rows, own, other):
    count, features = rows.shape
    half, deep = own.shape[1], features // STEPS
    return pl.pallas_call(
        functools.partial(forward_first_body, STEPS),
        grid=(STEPS,),
        in_specs=[
            pl.BlockSpec((count, deep), lambda i: (0, i)),
            pl.BlockSpec((deep, half), lambda i: (i, 0)),
            pl.BlockSpec((deep, half), lambda i: (i, 0)),
        ],
        out_specs=pl.BlockSpec((count, half), lambda i: (0, 0)),
        out_shape=jax.ShapeDtypeStruct((count, half), jnp.bfloat16),
        scratch_shapes=[pltpu.VMEM((count, 2 * half), jnp.float32)],
        compiler_params=pltpu.CompilerParams(vmem_limit_bytes=VMEM),
        cost_estimate=weigh(LATER * count * features * half),
    )(rows, own, other)


def forward_second_body(h_ref, own_ref, other_ref, out_ref):
    quarter = own_ref.shape[0]
    value = dot(h_ref[:, :quarter], own_ref[...]) + dot(h_ref[:, quarter:], other_ref[...])
    out_ref[...] = value.astype(jnp.bfloat16)


def forward_second(hidden, own, other):
    count, (quarter, features) = hidden.shape[0], own.shape
    wide = features // STEPS
    weight = pl.BlockSpec((quarter, wide), lambda i: (0, i))
    return pl.pallas_call(
        forward_second_body,
        grid=(STEPS,),
        in_specs=[pl.BlockSpec(hidden.shape, lambda i: (0, 0)), weight, weight],
        out_specs=pl.BlockSpec((count, wide), lambda i: (0, i)),
        out_shape=jax.ShapeDtypeStruct((count, features), jnp.bfloat16),
        compiler_params=pltpu.CompilerParams(vmem_limit_bytes=VMEM),
        cost_estimate=weigh(LATER * count * features * quarter),
    )(hidden, own, other)


def per_device(
    tokens_fwd,
    route_fwd,
    gate_fwd,
    grad_out,
    route_bwd,
    gate_bwd,
    saved_pre,
    w_in,
    w_down,
    att_grad,
):
    features = tokens_fwd.shape[1]
    owners = lax.axis_size("expert")
    pipes = lax.axis_size("pipe")
    experts = owners // ESPLIT
    capacity = saved_pre.shape[1] // owners
    quarter = w_down.shape[1]
    rows = experts * capacity
    weight_route, token_route = pair_routes(pipes, owners)
    groups = [[g * ESPLIT + x for g in range(experts)] for x in range(ESPLIT)]

    x = lax.axis_index("expert") % ESPLIT
    even = lax.axis_index("pipe") % 2 == 0
    near, far = x ^ 1, ESPLIT - 1 - x
    x_weight = jnp.where(even, near, far)
    x_token = jnp.where(even, far, near)
    x_cross = jnp.where(even, ESPLIT - 1 - x_weight, x_weight ^ 1)

    def swap_weights(v):
        return lax.ppermute(v, BOTH, weight_route)

    def swap_tokens(v):
        return lax.ppermute(v, BOTH, token_route)

    def exchange(v):
        return lax.all_to_all(
            v.reshape(experts, capacity, -1),
            "expert",
            split_axis=0,
            concat_axis=0,
            axis_index_groups=groups,
            tiled=True,
        ).reshape(rows, -1)

    def after(v, *others):
        return lax.optimization_barrier((v, *others))[0]

    buffer_bwd, select_bwd = dispatch(route_bwd, grad_out, experts, capacity, FIRST)
    own_bwd = exchange(buffer_bwd)

    down_own = w_down.reshape(quarter, features)
    down_other = swap_weights(down_own)
    buffer_fwd, select_fwd = dispatch(
        route_fwd, after(tokens_fwd, down_other), experts, capacity, BESIDE
    )
    saved = jnp.transpose(
        saved_pre.reshape(experts, ESPLIT, capacity, 2, quarter), (1, 3, 0, 2, 4)
    ).reshape(ESPLIT, 2, rows, quarter)

    def saved_of(column):
        return lax.dynamic_index_in_dim(saved, column, 0, keepdims=False)

    saved_out = jnp.stack([saved_of(x_weight), saved_of(x_cross)])
    saved_other = swap_weights(saved_out)
    in_own = w_in.reshape(features, 2 * quarter)
    in_other = swap_weights(in_own)

    own_bwd = after(own_bwd, buffer_fwd, saved_other, in_own)
    other_bwd = swap_tokens(own_bwd)
    own_fwd = exchange(after(buffer_fwd, own_bwd))
    mirrored = lax.ppermute(
        after(att_grad.astype(jnp.bfloat16), own_bwd),
        "pipe",
        [(p, pipes - 1 - p) for p in range(pipes)],
    )
    att_sum = att_grad + mirrored.astype(att_grad.dtype)

    def combine(select, arrived, gate):
        accum = lax.dot_general(
            select, arrived, (((0,), (0,)), ((), ())), preferred_element_type=jnp.float32
        )
        return (accum * gate).astype(jnp.bfloat16)

    near_d = backward_first(own_bwd, down_own, down_other, saved_of(x), saved_other[0])
    far_d = backward_first(other_bwd, down_own, down_other, saved_of(x_token), saved_other[1])
    far_d, near_d, own_fwd, in_other, _ = lax.optimization_barrier(
        (far_d, near_d, own_fwd, in_other, mirrored)
    )
    other_fwd = swap_tokens(own_fwd)
    far_bwd = backward_second(far_d, in_own, in_other)
    back = swap_tokens(far_bwd)
    near_bwd = backward_second(after(near_d, far_bwd), in_own, in_other)

    far_h = forward_first(after(other_fwd, near_bwd), in_own, in_other)
    far_fwd = forward_second(far_h, down_own, down_other)
    home = swap_tokens(far_fwd)
    near_h = forward_first(after(own_fwd, far_fwd), in_own, in_other)
    near_fwd = forward_second(near_h, down_own, down_other)

    def add(mine, partner):
        return (mine.astype(jnp.float32) + partner.astype(jnp.float32)).astype(jnp.bfloat16)

    total_bwd = add(near_bwd, back)
    arrived_bwd = exchange(total_bwd)
    arrived_fwd = exchange(add(near_fwd, after(home, total_bwd)))
    mixed_fwd = combine(select_fwd, arrived_fwd, gate_fwd)
    grad_in = combine(select_bwd, arrived_bwd, gate_bwd)
    return (mixed_fwd, grad_in, att_sum)


def solution(mesh):
    return jax.shard_map(
        per_device,
        mesh=mesh,
        in_specs=(
            P(("pipe", "expert"), None),
            P(("pipe", "expert"), None),
            P(("pipe", "expert"), None),
            P(("pipe", "expert"), None),
            P(("pipe", "expert"), None),
            P(("pipe", "expert"), None),
            P("pipe", None, None, "expert"),
            P("pipe", None, None, "expert"),
            P("pipe", "expert", None),
            P("pipe", "expert", None),
        ),
        out_specs=(
            P(("pipe", "expert"), None),
            P(("pipe", "expert"), None),
            P("pipe", "expert", None),
        ),
        check_vma=False,
    )
```

```python
import functools

import jax
import jax.numpy as jnp
from jax import lax
from jax.experimental import pallas as pl
from jax.experimental.pallas import tpu as pltpu
from jax.sharding import PartitionSpec as P

ESPLIT = 4
STEPS = 2
FIRST, LATER = 0.01, 0.01
BESIDE, BETWEEN = 300, 50
VMEM = 24 * 1024 * 1024
BOTH = ("pipe", "expert")


def pair_routes(pipes, owners):
    weights, tokens = [], []
    for p in range(pipes):
        for e in range(owners):
            x = e % ESPLIT
            near, far = e - x + (x ^ 1), e - x + (ESPLIT - 1 - x)
            here = p * owners + e
            weights.append((here, p * owners + (near if p % 2 == 0 else far)))
            tokens.append((here, p * owners + (far if p % 2 == 0 else near)))
    return weights, tokens


def weigh(work):
    return pl.CostEstimate(flops=int(work), bytes_accessed=int(work) // 128, transcendentals=0)


def dispatch_body(capacity, route_ref, rows_ref, buffer_ref, select_ref):
    route = route_ref[...]
    count = route.shape[1]
    slots = select_ref.shape[0]
    experts = lax.broadcasted_iota(jnp.int32, (8, count), 0)
    hits = jnp.concatenate(
        [(route == experts + 8 * k).astype(jnp.float32) for k in range(-(-slots // capacity // 8))]
    )
    earlier = lax.broadcasted_iota(jnp.int32, (count, count), 0) < lax.broadcasted_iota(
        jnp.int32, (count, count), 1
    )
    before = jnp.dot(
        hits.astype(jnp.bfloat16), earlier.astype(jnp.bfloat16), preferred_element_type=jnp.float32
    )
    slot = jnp.sum(before * hits, axis=0, keepdims=True).astype(jnp.int32)
    position = route * capacity + slot
    chosen = lax.broadcasted_iota(jnp.int32, (slots, count), 0) == position
    select = chosen.astype(jnp.float32).astype(jnp.bfloat16)
    select_ref[...] = select
    wide = rows_ref.shape[1] // 4
    for k in range(4):
        cols = slice(k * wide, (k + 1) * wide)
        buffer_ref[:, cols] = jnp.dot(
            select, rows_ref[:, cols], preferred_element_type=jnp.float32
        ).astype(jnp.bfloat16)


def dispatch(route, tokens, experts, capacity, scale):
    count, features = tokens.shape
    slots = experts * capacity
    return pl.pallas_call(
        functools.partial(dispatch_body, capacity),
        out_shape=(
            jax.ShapeDtypeStruct((slots, features), jnp.bfloat16),
            jax.ShapeDtypeStruct((slots, count), jnp.bfloat16),
        ),
        compiler_params=pltpu.CompilerParams(vmem_limit_bytes=VMEM),
        cost_estimate=weigh(scale * slots * count * features),
    )(route.reshape(1, count), tokens)


def dot(a, b):
    return jnp.dot(a, b, preferred_element_type=jnp.float32)


def dot_t(a, b):
    return lax.dot_general(a, b, (((1,), (1,)), ((), ())), preferred_element_type=jnp.float32)


def grad_of(d_hidden, gate_pre, up_pre):
    gate_pre, up_pre = gate_pre.astype(jnp.float32), up_pre.astype(jnp.float32)
    sig_gate = jax.nn.sigmoid(gate_pre)
    d_gate = d_hidden * up_pre * sig_gate * (1.0 + gate_pre * (1.0 - sig_gate))
    d_up = d_hidden * gate_pre * sig_gate
    return d_gate.astype(jnp.bfloat16), d_up.astype(jnp.bfloat16)


def backward_first_body(steps, rows_ref, own_ref, other_ref, stored_own, stored_other, out_ref, total):
    step = pl.program_id(0)

    @pl.when(step == 0)
    def _():
        total[...] = jnp.zeros_like(total)

    quarter = own_ref.shape[0]
    rows = rows_ref[...]
    total[:, :quarter] += dot_t(rows, own_ref[...])
    total[:, quarter:] += dot_t(rows, other_ref[...])

    @pl.when(step == steps - 1)
    def _():
        for k, stored in enumerate((stored_own, stored_other)):
            d_hidden = total[:, k * quarter : (k + 1) * quarter]
            d_gate, d_up = grad_of(d_hidden, stored[0], stored[1])
            out_ref[:, 2 * k * quarter : (2 * k + 1) * quarter] = d_gate
            out_ref[:, (2 * k + 1) * quarter : 2 * (k + 1) * quarter] = d_up


def backward_first(rows, own, other, stored_own, stored_other):
    count, features = rows.shape
    quarter, wide = own.shape[0], features // STEPS
    whole = pl.BlockSpec(stored_own.shape, lambda i: (0, 0, 0))
    return pl.pallas_call(
        functools.partial(backward_first_body, STEPS),
        grid=(STEPS,),
        in_specs=[
            pl.BlockSpec((count, wide), lambda i: (0, i)),
            pl.BlockSpec((quarter, wide), lambda i: (0, i)),
            pl.BlockSpec((quarter, wide), lambda i: (0, i)),
            whole,
            whole,
        ],
        out_specs=pl.BlockSpec((count, 4 * quarter), lambda i: (0, 0)),
        out_shape=jax.ShapeDtypeStruct((count, 4 * quarter), jnp.bfloat16),
        scratch_shapes=[pltpu.VMEM((count, 2 * quarter), jnp.float32)],
        compiler_params=pltpu.CompilerParams(vmem_limit_bytes=VMEM),
        cost_estimate=weigh(LATER * count * features * quarter),
    )(rows, own, other, stored_own, stored_other)


def backward_second_body(d_ref, weight_ref, *refs):
    value = dot_t(d_ref[...], weight_ref[...])
    if len(refs) == 2:
        value = value + refs[0][...].astype(jnp.float32)
    refs[-1][...] = value.astype(jnp.bfloat16)


def backward_second(d_pre, side, weight, cost, *addend):
    count, (features, half) = d_pre.shape[0], weight.shape
    wide = features // STEPS
    columns = pl.BlockSpec((count, wide), lambda i: (0, i))
    return pl.pallas_call(
        backward_second_body,
        grid=(STEPS,),
        in_specs=[
            pl.BlockSpec((count, half), lambda i: (0, side)),
            pl.BlockSpec((wide, half), lambda i: (i, 0)),
        ]
        + [columns] * len(addend),
        out_specs=columns,
        out_shape=jax.ShapeDtypeStruct((count, features), jnp.bfloat16),
        compiler_params=pltpu.CompilerParams(vmem_limit_bytes=VMEM),
        cost_estimate=weigh(cost * count * features * half),
    )(d_pre, weight, *addend)


def forward_first_body(steps, rows_ref, own_ref, other_ref, out_ref, total):
    step = pl.program_id(0)

    @pl.when(step == 0)
    def _():
        total[...] = jnp.zeros_like(total)

    half = own_ref.shape[1]
    rows = rows_ref[...]
    total[:, :half] += dot(rows, own_ref[...])
    total[:, half:] += dot(rows, other_ref[...])

    @pl.when(step == steps - 1)
    def _():
        quarter = half // 2
        for k in range(2):
            gate_pre = total[:, k * half : k * half + quarter]
            up_pre = total[:, k * half + quarter : (k + 1) * half]
            hidden = jax.nn.silu(gate_pre) * up_pre
            out_ref[:, k * quarter : (k + 1) * quarter] = hidden.astype(jnp.bfloat16)


def forward_first(rows, own, other, cost=LATER):
    count, features = rows.shape
    half, deep = own.shape[1], features // STEPS
    return pl.pallas_call(
        functools.partial(forward_first_body, STEPS),
        grid=(STEPS,),
        in_specs=[
            pl.BlockSpec((count, deep), lambda i: (0, i)),
            pl.BlockSpec((deep, half), lambda i: (i, 0)),
            pl.BlockSpec((deep, half), lambda i: (i, 0)),
        ],
        out_specs=pl.BlockSpec((count, half), lambda i: (0, 0)),
        out_shape=jax.ShapeDtypeStruct((count, half), jnp.bfloat16),
        scratch_shapes=[pltpu.VMEM((count, 2 * half), jnp.float32)],
        compiler_params=pltpu.CompilerParams(vmem_limit_bytes=VMEM),
        cost_estimate=weigh(cost * count * features * half),
    )(rows, own, other)


def forward_second_body(h_ref, own_ref, other_ref, out_ref):
    quarter = own_ref.shape[0]
    value = dot(h_ref[:, :quarter], own_ref[...]) + dot(h_ref[:, quarter:], other_ref[...])
    out_ref[...] = value.astype(jnp.bfloat16)


def forward_second(hidden, own, other):
    count, (quarter, features) = hidden.shape[0], own.shape
    wide = features // STEPS
    weight = pl.BlockSpec((quarter, wide), lambda i: (0, i))
    return pl.pallas_call(
        forward_second_body,
        grid=(STEPS,),
        in_specs=[pl.BlockSpec(hidden.shape, lambda i: (0, 0)), weight, weight],
        out_specs=pl.BlockSpec((count, wide), lambda i: (0, i)),
        out_shape=jax.ShapeDtypeStruct((count, features), jnp.bfloat16),
        compiler_params=pltpu.CompilerParams(vmem_limit_bytes=VMEM),
        cost_estimate=weigh(LATER * count * features * quarter),
    )(hidden, own, other)


def per_device(
    tokens_fwd,
    route_fwd,
    gate_fwd,
    grad_out,
    route_bwd,
    gate_bwd,
    saved_pre,
    w_in,
    w_down,
    att_grad,
):
    features = tokens_fwd.shape[1]
    owners = lax.axis_size("expert")
    pipes = lax.axis_size("pipe")
    experts = owners // ESPLIT
    capacity = saved_pre.shape[1] // owners
    quarter = w_down.shape[1]
    rows = experts * capacity
    weight_route, token_route = pair_routes(pipes, owners)
    groups = [[g * ESPLIT + x for g in range(experts)] for x in range(ESPLIT)]

    x = lax.axis_index("expert") % ESPLIT
    even = lax.axis_index("pipe") % 2 == 0
    near, far = x ^ 1, ESPLIT - 1 - x
    x_weight = jnp.where(even, near, far)
    x_token = jnp.where(even, far, near)
    x_cross = jnp.where(even, ESPLIT - 1 - x_weight, x_weight ^ 1)

    def swap_weights(v):
        return lax.ppermute(v, BOTH, weight_route)

    def swap_tokens(v):
        return lax.ppermute(v, BOTH, token_route)

    def exchange(v):
        return lax.all_to_all(
            v.reshape(experts, -1, features),
            "expert",
            split_axis=0,
            concat_axis=0,
            axis_index_groups=groups,
            tiled=True,
        ).reshape(-1, features)

    def after(v, *others):
        return lax.optimization_barrier((v, *others))[0]

    buffer_bwd, select_bwd = dispatch(route_bwd, grad_out, experts, capacity, FIRST)
    own_bwd = exchange(buffer_bwd)
    select_far = swap_tokens(select_bwd)

    down_own = w_down.reshape(quarter, features)
    down_other = swap_weights(down_own)
    buffer_fwd, select_fwd = dispatch(
        route_fwd, after(tokens_fwd, down_other), experts, capacity, BESIDE
    )
    saved = jnp.transpose(
        saved_pre.reshape(experts, ESPLIT, capacity, 2, quarter), (1, 3, 0, 2, 4)
    ).reshape(ESPLIT, 2, rows, quarter)

    def saved_of(column):
        return lax.dynamic_index_in_dim(saved, column, 0, keepdims=False)

    saved_out = jnp.stack([saved_of(x_weight), saved_of(x_cross)])
    saved_other = swap_weights(saved_out)
    in_own = w_in.reshape(features, 2 * quarter)
    in_other = swap_weights(in_own)

    own_bwd = after(own_bwd, buffer_fwd, saved_other, in_own)
    other_bwd = swap_tokens(own_bwd)
    own_fwd = exchange(after(buffer_fwd, own_bwd))
    mirrored = lax.ppermute(
        after(att_grad.astype(jnp.bfloat16), own_bwd),
        "pipe",
        [(p, pipes - 1 - p) for p in range(pipes)],
    )
    att_sum = att_grad + mirrored.astype(att_grad.dtype)

    def combine(select, arrived, gate):
        accum = lax.dot_general(
            select, arrived, (((0,), (0,)), ((), ())), preferred_element_type=jnp.float32
        )
        return (accum * gate).astype(jnp.bfloat16)

    near_d = backward_first(own_bwd, down_own, down_other, saved_of(x), saved_other[0])
    far_d = backward_first(other_bwd, down_own, down_other, saved_of(x_token), saved_other[1])
    def beside(mine, partner):
        pair = (mine.reshape(experts, capacity, -1), partner.reshape(experts, capacity, -1))
        return jnp.concatenate(pair, axis=1).reshape(2 * rows, -1)

    both_d = beside(near_d, far_d)
    both_own = backward_second(both_d, 0, in_own, LATER)
    both_d, both_own, own_fwd, in_other, select_far, _ = lax.optimization_barrier(
        (both_d, both_own, own_fwd, in_other, select_far, mirrored)
    )
    other_fwd = swap_tokens(own_fwd)
    both_bwd = backward_second(both_d, 1, in_other, BESIDE, both_own)
    arrived_bwd = exchange(both_bwd)

    far_h = forward_first(after(other_fwd, both_bwd), in_own, in_other, BETWEEN)
    far_fwd = forward_second(far_h, down_own, down_other)
    home = swap_tokens(far_fwd)
    near_h = forward_first(after(own_fwd, far_fwd), in_own, in_other)
    near_fwd = forward_second(near_h, down_own, down_other)
    total_fwd = (near_fwd.astype(jnp.float32) + home.astype(jnp.float32)).astype(jnp.bfloat16)
    arrived_fwd = exchange(after(total_fwd, arrived_bwd))
    mixed_fwd = combine(select_fwd, arrived_fwd, gate_fwd)

    blank = jnp.zeros_like(select_bwd)

    def rows_of(select):
        return lax.dot_general(
            select, arrived_bwd, (((0,), (0,)), ((), ())), preferred_element_type=jnp.float32
        )

    back = swap_tokens(rows_of(beside(blank, select_far)).astype(jnp.bfloat16))
    mine = lax.optimization_barrier(rows_of(beside(select_bwd, blank)))
    grad_in = ((mine + back.astype(jnp.float32)) * gate_bwd).astype(jnp.bfloat16)
    return (mixed_fwd, grad_in, att_sum)


def solution(mesh):
    return jax.shard_map(
        per_device,
        mesh=mesh,
        in_specs=(
            P(("pipe", "expert"), None),
            P(("pipe", "expert"), None),
            P(("pipe", "expert"), None),
            P(("pipe", "expert"), None),
            P(("pipe", "expert"), None),
            P(("pipe", "expert"), None),
            P("pipe", None, None, "expert"),
            P("pipe", None, None, "expert"),
            P("pipe", "expert", None),
            P("pipe", "expert", None),
        ),
        out_specs=(
            P(("pipe", "expert"), None),
            P(("pipe", "expert"), None),
            P("pipe", "expert", None),
        ),
        check_vma=False,
    )
```

```python
import functools

import jax
import jax.numpy as jnp
from jax import lax
from jax.experimental import pallas as pl
from jax.experimental.pallas import tpu as pltpu
from jax.sharding import PartitionSpec as P

ESPLIT = 4
STEPS = 2
FIRST, LATER = 0.01, 0.01
BESIDE, BETWEEN = 300, 50
VMEM, WIDE = 24 * 1024 * 1024, 56 * 1024 * 1024
BOTH = ("pipe", "expert")


def pair_routes(pipes, owners):
    weights, tokens = [], []
    for p in range(pipes):
        for e in range(owners):
            x = e % ESPLIT
            near, far = e - x + (x ^ 1), e - x + (ESPLIT - 1 - x)
            here = p * owners + e
            weights.append((here, p * owners + (near if p % 2 == 0 else far)))
            tokens.append((here, p * owners + (far if p % 2 == 0 else near)))
    return weights, tokens


def weigh(work):
    return pl.CostEstimate(flops=int(work), bytes_accessed=int(work) // 128, transcendentals=0)


def dispatch_body(capacity, route_ref, rows_ref, buffer_ref, select_ref):
    route = route_ref[...]
    count = route.shape[1]
    slots = select_ref.shape[0]
    experts = lax.broadcasted_iota(jnp.int32, (8, count), 0)
    hits = jnp.concatenate(
        [(route == experts + 8 * k).astype(jnp.float32) for k in range(-(-slots // capacity // 8))]
    )
    earlier = lax.broadcasted_iota(jnp.int32, (count, count), 0) < lax.broadcasted_iota(
        jnp.int32, (count, count), 1
    )
    before = jnp.dot(
        hits.astype(jnp.bfloat16), earlier.astype(jnp.bfloat16), preferred_element_type=jnp.float32
    )
    slot = jnp.sum(before * hits, axis=0, keepdims=True).astype(jnp.int32)
    position = route * capacity + slot
    chosen = lax.broadcasted_iota(jnp.int32, (slots, count), 0) == position
    select = chosen.astype(jnp.float32).astype(jnp.bfloat16)
    select_ref[...] = select
    wide = rows_ref.shape[1] // 4
    for k in range(4):
        cols = slice(k * wide, (k + 1) * wide)
        buffer_ref[:, cols] = jnp.dot(
            select, rows_ref[:, cols], preferred_element_type=jnp.float32
        ).astype(jnp.bfloat16)


def dispatch(route, tokens, experts, capacity, scale):
    count, features = tokens.shape
    slots = experts * capacity
    return pl.pallas_call(
        functools.partial(dispatch_body, capacity),
        out_shape=(
            jax.ShapeDtypeStruct((slots, features), jnp.bfloat16),
            jax.ShapeDtypeStruct((slots, count), jnp.bfloat16),
        ),
        compiler_params=pltpu.CompilerParams(vmem_limit_bytes=VMEM),
        cost_estimate=weigh(scale * slots * count * features),
    )(route.reshape(1, count), tokens)


def dot(a, b):
    return jnp.dot(a, b, preferred_element_type=jnp.float32)


def dot_t(a, b):
    return lax.dot_general(a, b, (((1,), (1,)), ((), ())), preferred_element_type=jnp.float32)


def grad_of(d_hidden, gate_pre, up_pre):
    gate_pre, up_pre = gate_pre.astype(jnp.float32), up_pre.astype(jnp.float32)
    sig_gate = jax.nn.sigmoid(gate_pre)
    d_gate = d_hidden * up_pre * sig_gate * (1.0 + gate_pre * (1.0 - sig_gate))
    d_up = d_hidden * gate_pre * sig_gate
    return d_gate.astype(jnp.bfloat16), d_up.astype(jnp.bfloat16)


def backward_first_body(steps, rows_ref, own_ref, other_ref, stored_own, stored_other, out_ref, total):
    step = pl.program_id(0)

    @pl.when(step == 0)
    def _():
        total[...] = jnp.zeros_like(total)

    quarter = own_ref.shape[0]
    rows = rows_ref[...]
    total[:, :quarter] += dot_t(rows, own_ref[...])
    total[:, quarter:] += dot_t(rows, other_ref[...])

    @pl.when(step == steps - 1)
    def _():
        for k, stored in enumerate((stored_own, stored_other)):
            d_hidden = total[:, k * quarter : (k + 1) * quarter]
            d_gate, d_up = grad_of(d_hidden, stored[0], stored[1])
            out_ref[:, 2 * k * quarter : (2 * k + 1) * quarter] = d_gate
            out_ref[:, (2 * k + 1) * quarter : 2 * (k + 1) * quarter] = d_up


def backward_first(rows, own, other, stored_own, stored_other):
    count, features = rows.shape
    quarter, wide = own.shape[0], features // STEPS
    whole = pl.BlockSpec(stored_own.shape, lambda i: (0, 0, 0))
    return pl.pallas_call(
        functools.partial(backward_first_body, STEPS),
        grid=(STEPS,),
        in_specs=[
            pl.BlockSpec((count, wide), lambda i: (0, i)),
            pl.BlockSpec((quarter, wide), lambda i: (0, i)),
            pl.BlockSpec((quarter, wide), lambda i: (0, i)),
            whole,
            whole,
        ],
        out_specs=pl.BlockSpec((count, 4 * quarter), lambda i: (0, 0)),
        out_shape=jax.ShapeDtypeStruct((count, 4 * quarter), jnp.bfloat16),
        scratch_shapes=[pltpu.VMEM((count, 2 * quarter), jnp.float32)],
        compiler_params=pltpu.CompilerParams(vmem_limit_bytes=VMEM),
        cost_estimate=weigh(LATER * count * features * quarter),
    )(rows, own, other, stored_own, stored_other)


def backward_second_body(d_ref, weight_ref, *refs):
    value = dot_t(d_ref[...], weight_ref[...])
    if len(refs) == 2:
        value = value + refs[0][...].astype(jnp.float32)
    refs[-1][...] = value.astype(jnp.bfloat16)


def backward_second(d_pre, side, weight, cost, *addend):
    count, (features, half) = d_pre.shape[0], weight.shape
    wide = features // STEPS
    columns = pl.BlockSpec((count, wide), lambda i: (0, i))
    return pl.pallas_call(
        backward_second_body,
        grid=(STEPS,),
        in_specs=[
            pl.BlockSpec((count, half), lambda i: (0, side)),
            pl.BlockSpec((wide, half), lambda i: (i, 0)),
        ]
        + [columns] * len(addend),
        out_specs=columns,
        out_shape=jax.ShapeDtypeStruct((count, features), jnp.bfloat16),
        compiler_params=pltpu.CompilerParams(vmem_limit_bytes=WIDE),
        cost_estimate=weigh(cost * count * features * half),
    )(d_pre, weight, *addend)


def forward_first_body(steps, rows_ref, own_ref, other_ref, out_ref, total):
    step = pl.program_id(0)

    @pl.when(step == 0)
    def _():
        total[...] = jnp.zeros_like(total)

    half = own_ref.shape[1]
    rows = rows_ref[...]
    total[:, :half] += dot(rows, own_ref[...])
    total[:, half:] += dot(rows, other_ref[...])

    @pl.when(step == steps - 1)
    def _():
        quarter = half // 2
        for k in range(2):
            gate_pre = total[:, k * half : k * half + quarter]
            up_pre = total[:, k * half + quarter : (k + 1) * half]
            hidden = jax.nn.silu(gate_pre) * up_pre
            out_ref[:, k * quarter : (k + 1) * quarter] = hidden.astype(jnp.bfloat16)


def forward_first(rows, own, other, cost=LATER):
    count, features = rows.shape
    half, deep = own.shape[1], features // STEPS
    return pl.pallas_call(
        functools.partial(forward_first_body, STEPS),
        grid=(STEPS,),
        in_specs=[
            pl.BlockSpec((count, deep), lambda i: (0, i)),
            pl.BlockSpec((deep, half), lambda i: (i, 0)),
            pl.BlockSpec((deep, half), lambda i: (i, 0)),
        ],
        out_specs=pl.BlockSpec((count, half), lambda i: (0, 0)),
        out_shape=jax.ShapeDtypeStruct((count, half), jnp.bfloat16),
        scratch_shapes=[pltpu.VMEM((count, 2 * half), jnp.float32)],
        compiler_params=pltpu.CompilerParams(vmem_limit_bytes=VMEM),
        cost_estimate=weigh(cost * count * features * half),
    )(rows, own, other)


def forward_second_body(h_ref, own_ref, other_ref, out_ref):
    quarter = own_ref.shape[0]
    value = dot(h_ref[:, :quarter], own_ref[...]) + dot(h_ref[:, quarter:], other_ref[...])
    out_ref[...] = value.astype(jnp.bfloat16)


def forward_second(hidden, own, other):
    count, (quarter, features) = hidden.shape[0], own.shape
    wide = features // STEPS
    weight = pl.BlockSpec((quarter, wide), lambda i: (0, i))
    return pl.pallas_call(
        forward_second_body,
        grid=(STEPS,),
        in_specs=[pl.BlockSpec(hidden.shape, lambda i: (0, 0)), weight, weight],
        out_specs=pl.BlockSpec((count, wide), lambda i: (0, i)),
        out_shape=jax.ShapeDtypeStruct((count, features), jnp.bfloat16),
        compiler_params=pltpu.CompilerParams(vmem_limit_bytes=VMEM),
        cost_estimate=weigh(LATER * count * features * quarter),
    )(hidden, own, other)


def per_device(
    tokens_fwd,
    route_fwd,
    gate_fwd,
    grad_out,
    route_bwd,
    gate_bwd,
    saved_pre,
    w_in,
    w_down,
    att_grad,
):
    features = tokens_fwd.shape[1]
    owners = lax.axis_size("expert")
    pipes = lax.axis_size("pipe")
    experts = owners // ESPLIT
    capacity = saved_pre.shape[1] // owners
    quarter = w_down.shape[1]
    rows = experts * capacity
    weight_route, token_route = pair_routes(pipes, owners)
    groups = [[g * ESPLIT + x for g in range(experts)] for x in range(ESPLIT)]

    x = lax.axis_index("expert") % ESPLIT
    even = lax.axis_index("pipe") % 2 == 0
    near, far = x ^ 1, ESPLIT - 1 - x
    x_weight = jnp.where(even, near, far)
    x_token = jnp.where(even, far, near)
    x_cross = jnp.where(even, ESPLIT - 1 - x_weight, x_weight ^ 1)

    def swap_weights(v):
        return lax.ppermute(v, BOTH, weight_route)

    def swap_tokens(v):
        return lax.ppermute(v, BOTH, token_route)

    def exchange(v):
        return lax.all_to_all(
            v.reshape(experts, -1, features),
            "expert",
            split_axis=0,
            concat_axis=0,
            axis_index_groups=groups,
            tiled=True,
        ).reshape(-1, features)

    def after(v, *others):
        return lax.optimization_barrier((v, *others))[0]

    buffer_bwd, select_bwd = dispatch(route_bwd, grad_out, experts, capacity, FIRST)
    own_bwd = exchange(buffer_bwd)
    select_far = swap_tokens(select_bwd)

    down_own = w_down.reshape(quarter, features)
    down_other = swap_weights(down_own)
    buffer_fwd, select_fwd = dispatch(
        route_fwd, after(tokens_fwd, down_other), experts, capacity, BESIDE
    )
    saved = jnp.transpose(
        saved_pre.reshape(experts, ESPLIT, capacity, 2, quarter), (1, 3, 0, 2, 4)
    ).reshape(ESPLIT, 2, rows, quarter)

    def saved_of(column):
        return lax.dynamic_index_in_dim(saved, column, 0, keepdims=False)

    saved_out = jnp.stack([saved_of(x_weight), saved_of(x_cross)])
    saved_other = swap_weights(saved_out)
    in_own = w_in.reshape(features, 2 * quarter)
    in_other = swap_weights(in_own)

    own_bwd = after(own_bwd, buffer_fwd, saved_other, in_own)
    other_bwd = swap_tokens(own_bwd)
    own_fwd = exchange(after(buffer_fwd, own_bwd))
    mirrored = lax.ppermute(
        after(att_grad.astype(jnp.bfloat16), own_bwd),
        "pipe",
        [(p, pipes - 1 - p) for p in range(pipes)],
    )
    att_sum = att_grad + mirrored.astype(att_grad.dtype)

    def combine(select, arrived, gate):
        accum = lax.dot_general(
            select, arrived, (((0,), (0,)), ((), ())), preferred_element_type=jnp.float32
        )
        return (accum * gate).astype(jnp.bfloat16)

    near_d = backward_first(own_bwd, down_own, down_other, saved_of(x), saved_other[0])
    far_d = backward_first(other_bwd, down_own, down_other, saved_of(x_token), saved_other[1])
    def beside(mine, partner):
        pair = (mine.reshape(experts, capacity, -1), partner.reshape(experts, capacity, -1))
        return jnp.concatenate(pair, axis=1).reshape(2 * rows, -1)

    both_d = beside(near_d, far_d)
    both_own = backward_second(both_d, 0, in_own, LATER)
    both_d, both_own, own_fwd, in_other, select_far, _ = lax.optimization_barrier(
        (both_d, both_own, own_fwd, in_other, select_far, mirrored)
    )
    other_fwd = swap_tokens(own_fwd)
    both_bwd = backward_second(both_d, 1, in_other, BESIDE, both_own)
    arrived_bwd = exchange(both_bwd)

    far_h = forward_first(after(other_fwd, both_bwd), in_own, in_other, BETWEEN)
    far_fwd = forward_second(far_h, down_own, down_other)
    home = swap_tokens(far_fwd)
    near_h = forward_first(after(own_fwd, far_fwd), in_own, in_other)
    near_fwd = forward_second(near_h, down_own, down_other)
    total_fwd = (near_fwd.astype(jnp.float32) + home.astype(jnp.float32)).astype(jnp.bfloat16)
    arrived_fwd = exchange(after(total_fwd, arrived_bwd))
    mixed_fwd = combine(select_fwd, arrived_fwd, gate_fwd)

    blank = jnp.zeros_like(select_bwd)

    def rows_of(select):
        return lax.dot_general(
            select, arrived_bwd, (((0,), (0,)), ((), ())), preferred_element_type=jnp.float32
        )

    back = swap_tokens(rows_of(beside(blank, select_far)).astype(jnp.bfloat16))
    mine = lax.optimization_barrier(rows_of(beside(select_bwd, blank)))
    grad_in = ((mine + back.astype(jnp.float32)) * gate_bwd).astype(jnp.bfloat16)
    return (mixed_fwd, grad_in, att_sum)


def solution(mesh):
    return jax.shard_map(
        per_device,
        mesh=mesh,
        in_specs=(
            P(("pipe", "expert"), None),
            P(("pipe", "expert"), None),
            P(("pipe", "expert"), None),
            P(("pipe", "expert"), None),
            P(("pipe", "expert"), None),
            P(("pipe", "expert"), None),
            P("pipe", None, None, "expert"),
            P("pipe", None, None, "expert"),
            P("pipe", "expert", None),
            P("pipe", "expert", None),
        ),
        out_specs=(
            P(("pipe", "expert"), None),
            P(("pipe", "expert"), None),
            P("pipe", "expert", None),
        ),
        check_vma=False,
    )
```

```python
import functools

import jax
import jax.numpy as jnp
from jax import lax
from jax.experimental import pallas as pl
from jax.experimental.pallas import tpu as pltpu
from jax.sharding import PartitionSpec as P

ESPLIT = 4
STEPS = 2
FIRST, LATER = 0.01, 0.01
BESIDE, BETWEEN = 300, 50
VMEM, WIDE = 24 * 1024 * 1024, 56 * 1024 * 1024
BOTH = ("pipe", "expert")


def pair_routes(pipes, owners):
    weights, tokens = [], []
    for p in range(pipes):
        for e in range(owners):
            x = e % ESPLIT
            near, far = e - x + (x ^ 1), e - x + (ESPLIT - 1 - x)
            here = p * owners + e
            weights.append((here, p * owners + (near if p % 2 == 0 else far)))
            tokens.append((here, p * owners + (far if p % 2 == 0 else near)))
    return weights, tokens


def weigh(work):
    return pl.CostEstimate(flops=int(work), bytes_accessed=int(work) // 128, transcendentals=0)


def dispatch_body(capacity, route_ref, rows_ref, buffer_ref, select_ref):
    route = route_ref[...]
    count = route.shape[1]
    slots = select_ref.shape[0]
    experts = lax.broadcasted_iota(jnp.int32, (8, count), 0)
    hits = jnp.concatenate(
        [(route == experts + 8 * k).astype(jnp.float32) for k in range(-(-slots // capacity // 8))]
    )
    earlier = lax.broadcasted_iota(jnp.int32, (count, count), 0) < lax.broadcasted_iota(
        jnp.int32, (count, count), 1
    )
    before = jnp.dot(
        hits.astype(jnp.bfloat16), earlier.astype(jnp.bfloat16), preferred_element_type=jnp.float32
    )
    slot = jnp.sum(before * hits, axis=0, keepdims=True).astype(jnp.int32)
    position = route * capacity + slot
    chosen = lax.broadcasted_iota(jnp.int32, (slots, count), 0) == position
    select = chosen.astype(jnp.float32).astype(jnp.bfloat16)
    select_ref[...] = select
    wide = rows_ref.shape[1] // 4
    for k in range(4):
        cols = slice(k * wide, (k + 1) * wide)
        buffer_ref[:, cols] = jnp.dot(
            select, rows_ref[:, cols], preferred_element_type=jnp.float32
        ).astype(jnp.bfloat16)


def dispatch(route, tokens, experts, capacity, scale):
    count, features = tokens.shape
    slots = experts * capacity
    return pl.pallas_call(
        functools.partial(dispatch_body, capacity),
        out_shape=(
            jax.ShapeDtypeStruct((slots, features), jnp.bfloat16),
            jax.ShapeDtypeStruct((slots, count), jnp.bfloat16),
        ),
        compiler_params=pltpu.CompilerParams(vmem_limit_bytes=VMEM),
        cost_estimate=weigh(scale * slots * count * features),
    )(route.reshape(1, count), tokens)


def dot(a, b):
    return jnp.dot(a, b, preferred_element_type=jnp.float32)


def dot_t(a, b):
    return lax.dot_general(a, b, (((1,), (1,)), ((), ())), preferred_element_type=jnp.float32)


def grad_of(d_hidden, gate_pre, up_pre):
    gate_pre, up_pre = gate_pre.astype(jnp.float32), up_pre.astype(jnp.float32)
    sig_gate = jax.nn.sigmoid(gate_pre)
    d_gate = d_hidden * up_pre * sig_gate * (1.0 + gate_pre * (1.0 - sig_gate))
    d_up = d_hidden * gate_pre * sig_gate
    return d_gate.astype(jnp.bfloat16), d_up.astype(jnp.bfloat16)


def backward_first_body(steps, rows_ref, own_ref, other_ref, stored_own, stored_other, out_ref, total):
    step = pl.program_id(0)

    @pl.when(step == 0)
    def _():
        total[...] = jnp.zeros_like(total)

    quarter = own_ref.shape[0]
    rows = rows_ref[...]
    total[:, :quarter] += dot_t(rows, own_ref[...])
    total[:, quarter:] += dot_t(rows, other_ref[...])

    @pl.when(step == steps - 1)
    def _():
        for k, stored in enumerate((stored_own, stored_other)):
            d_hidden = total[:, k * quarter : (k + 1) * quarter]
            d_gate, d_up = grad_of(d_hidden, stored[0], stored[1])
            out_ref[:, 2 * k * quarter : (2 * k + 1) * quarter] = d_gate
            out_ref[:, (2 * k + 1) * quarter : 2 * (k + 1) * quarter] = d_up


def backward_first(rows, own, other, stored_own, stored_other):
    count, features = rows.shape
    quarter, wide = own.shape[0], features // STEPS
    whole = pl.BlockSpec(stored_own.shape, lambda i: (0, 0, 0))
    return pl.pallas_call(
        functools.partial(backward_first_body, STEPS),
        grid=(STEPS,),
        in_specs=[
            pl.BlockSpec((count, wide), lambda i: (0, i)),
            pl.BlockSpec((quarter, wide), lambda i: (0, i)),
            pl.BlockSpec((quarter, wide), lambda i: (0, i)),
            whole,
            whole,
        ],
        out_specs=pl.BlockSpec((count, 4 * quarter), lambda i: (0, 0)),
        out_shape=jax.ShapeDtypeStruct((count, 4 * quarter), jnp.bfloat16),
        scratch_shapes=[pltpu.VMEM((count, 2 * quarter), jnp.float32)],
        compiler_params=pltpu.CompilerParams(vmem_limit_bytes=VMEM),
        cost_estimate=weigh(LATER * count * features * quarter),
    )(rows, own, other, stored_own, stored_other)


def backward_second_body(d_ref, weight_ref, *refs):
    value = dot_t(d_ref[...], weight_ref[...])
    if len(refs) == 2:
        value = value + refs[0][...].astype(jnp.float32)
    refs[-1][...] = value.astype(jnp.bfloat16)


def backward_second(d_pre, side, weight, cost, *addend):
    count, (features, half) = d_pre.shape[0], weight.shape
    wide = features // STEPS
    columns = pl.BlockSpec((count, wide), lambda i: (0, i))
    return pl.pallas_call(
        backward_second_body,
        grid=(STEPS,),
        in_specs=[
            pl.BlockSpec((count, half), lambda i: (0, side)),
            pl.BlockSpec((wide, half), lambda i: (i, 0)),
        ]
        + [columns] * len(addend),
        out_specs=columns,
        out_shape=jax.ShapeDtypeStruct((count, features), jnp.bfloat16),
        compiler_params=pltpu.CompilerParams(vmem_limit_bytes=WIDE),
        cost_estimate=weigh(cost * count * features * half),
    )(d_pre, weight, *addend)


def forward_first_body(steps, rows_ref, own_ref, other_ref, out_ref, total):
    step = pl.program_id(0)

    @pl.when(step == 0)
    def _():
        total[...] = jnp.zeros_like(total)

    half = own_ref.shape[1]
    rows = rows_ref[...]
    total[:, :half] += dot(rows, own_ref[...])
    total[:, half:] += dot(rows, other_ref[...])

    @pl.when(step == steps - 1)
    def _():
        quarter = half // 2
        for k in range(2):
            gate_pre = total[:, k * half : k * half + quarter]
            up_pre = total[:, k * half + quarter : (k + 1) * half]
            hidden = jax.nn.silu(gate_pre) * up_pre
            out_ref[:, k * quarter : (k + 1) * quarter] = hidden.astype(jnp.bfloat16)


def forward_first(rows, own, other, cost=LATER):
    count, features = rows.shape
    half, deep = own.shape[1], features // STEPS
    return pl.pallas_call(
        functools.partial(forward_first_body, STEPS),
        grid=(STEPS,),
        in_specs=[
            pl.BlockSpec((count, deep), lambda i: (0, i)),
            pl.BlockSpec((deep, half), lambda i: (i, 0)),
            pl.BlockSpec((deep, half), lambda i: (i, 0)),
        ],
        out_specs=pl.BlockSpec((count, half), lambda i: (0, 0)),
        out_shape=jax.ShapeDtypeStruct((count, half), jnp.bfloat16),
        scratch_shapes=[pltpu.VMEM((count, 2 * half), jnp.float32)],
        compiler_params=pltpu.CompilerParams(vmem_limit_bytes=VMEM),
        cost_estimate=weigh(cost * count * features * half),
    )(rows, own, other)


def forward_second_body(h_ref, own_ref, other_ref, out_ref):
    quarter = own_ref.shape[0]
    value = dot(h_ref[:, :quarter], own_ref[...]) + dot(h_ref[:, quarter:], other_ref[...])
    out_ref[...] = value.astype(jnp.bfloat16)


def forward_second(hidden, own, other):
    count, (quarter, features) = hidden.shape[0], own.shape
    wide = features // STEPS
    weight = pl.BlockSpec((quarter, wide), lambda i: (0, i))
    return pl.pallas_call(
        forward_second_body,
        grid=(STEPS,),
        in_specs=[pl.BlockSpec(hidden.shape, lambda i: (0, 0)), weight, weight],
        out_specs=pl.BlockSpec((count, wide), lambda i: (0, i)),
        out_shape=jax.ShapeDtypeStruct((count, features), jnp.bfloat16),
        compiler_params=pltpu.CompilerParams(vmem_limit_bytes=VMEM),
        cost_estimate=weigh(LATER * count * features * quarter),
    )(hidden, own, other)


def per_device(
    tokens_fwd,
    route_fwd,
    gate_fwd,
    grad_out,
    route_bwd,
    gate_bwd,
    saved_pre,
    w_in,
    w_down,
    att_grad,
):
    features = tokens_fwd.shape[1]
    owners = lax.axis_size("expert")
    pipes = lax.axis_size("pipe")
    experts = owners // ESPLIT
    capacity = saved_pre.shape[1] // owners
    quarter = w_down.shape[1]
    rows = experts * capacity
    weight_route, token_route = pair_routes(pipes, owners)
    groups = [[g * ESPLIT + x for g in range(experts)] for x in range(ESPLIT)]

    x = lax.axis_index("expert") % ESPLIT
    even = lax.axis_index("pipe") % 2 == 0
    near, far = x ^ 1, ESPLIT - 1 - x
    x_weight = jnp.where(even, near, far)
    x_token = jnp.where(even, far, near)
    x_cross = jnp.where(even, ESPLIT - 1 - x_weight, x_weight ^ 1)

    def swap_weights(v):
        return lax.ppermute(v, BOTH, weight_route)

    def swap_tokens(v):
        return lax.ppermute(v, BOTH, token_route)

    def exchange(v):
        return lax.all_to_all(
            v.reshape(experts, -1, features),
            "expert",
            split_axis=0,
            concat_axis=0,
            axis_index_groups=groups,
            tiled=True,
        ).reshape(-1, features)

    def after(v, *others):
        return lax.optimization_barrier((v, *others))[0]

    buffer_bwd, select_bwd = dispatch(route_bwd, grad_out, experts, capacity, FIRST)
    own_bwd = exchange(buffer_bwd)
    select_far = swap_tokens(select_bwd)

    down_own = w_down.reshape(quarter, features)
    down_other = swap_weights(down_own)
    buffer_fwd, select_fwd = dispatch(
        route_fwd, after(tokens_fwd, down_other), experts, capacity, BESIDE
    )
    saved = jnp.transpose(
        saved_pre.reshape(experts, ESPLIT, capacity, 2, quarter), (1, 3, 0, 2, 4)
    ).reshape(ESPLIT, 2, rows, quarter)

    def saved_of(column):
        return lax.dynamic_index_in_dim(saved, column, 0, keepdims=False)

    saved_out = jnp.stack([saved_of(x_weight), saved_of(x_cross)])
    saved_other = swap_weights(saved_out)
    in_own = w_in.reshape(features, 2 * quarter)
    in_other = swap_weights(in_own)

    own_bwd = after(own_bwd, buffer_fwd, saved_other, in_own)
    other_bwd = swap_tokens(own_bwd)
    own_fwd = exchange(after(buffer_fwd, own_bwd))
    mirrored = lax.ppermute(
        after(att_grad.astype(jnp.bfloat16), own_bwd),
        "pipe",
        [(p, pipes - 1 - p) for p in range(pipes)],
    )
    att_sum = att_grad + mirrored.astype(att_grad.dtype)

    def combine(select, arrived, gate):
        accum = lax.dot_general(
            select, arrived, (((0,), (0,)), ((), ())), preferred_element_type=jnp.float32
        )
        return (accum * gate).astype(jnp.bfloat16)

    near_d = backward_first(own_bwd, down_own, down_other, saved_of(x), saved_other[0])
    far_d = backward_first(other_bwd, down_own, down_other, saved_of(x_token), saved_other[1])
    def beside(mine, partner):
        pair = (mine.reshape(experts, capacity, -1), partner.reshape(experts, capacity, -1))
        return jnp.concatenate(pair, axis=1).reshape(2 * rows, -1)

    both_d = beside(near_d, far_d)
    both_own = backward_second(both_d, 0, in_own, LATER)
    blank = jnp.zeros_like(select_bwd)
    picks = (beside(blank, select_far), beside(select_bwd, blank))
    both_d, both_own, own_fwd, in_other, picks, _ = lax.optimization_barrier(
        (both_d, both_own, own_fwd, in_other, picks, mirrored)
    )
    other_fwd = swap_tokens(own_fwd)
    both_bwd = backward_second(both_d, 1, in_other, BESIDE, both_own)
    arrived_bwd = exchange(both_bwd)

    far_h = forward_first(after(other_fwd, both_bwd), in_own, in_other, BETWEEN)
    far_fwd = forward_second(far_h, down_own, down_other)
    home = swap_tokens(far_fwd)
    near_h = forward_first(after(own_fwd, far_fwd), in_own, in_other)
    near_fwd = forward_second(near_h, down_own, down_other)
    total_fwd = (near_fwd.astype(jnp.float32) + home.astype(jnp.float32)).astype(jnp.bfloat16)
    arrived_fwd = exchange(after(total_fwd, arrived_bwd))
    mixed_fwd = combine(select_fwd, arrived_fwd, gate_fwd)

    def rows_of(select):
        return lax.dot_general(
            select, arrived_bwd, (((0,), (0,)), ((), ())), preferred_element_type=jnp.float32
        )

    back = swap_tokens(rows_of(picks[0]).astype(jnp.bfloat16))
    mine = lax.optimization_barrier(rows_of(picks[1]))
    grad_in = ((mine + back.astype(jnp.float32)) * gate_bwd).astype(jnp.bfloat16)
    return (mixed_fwd, grad_in, att_sum)


def solution(mesh):
    return jax.shard_map(
        per_device,
        mesh=mesh,
        in_specs=(
            P(("pipe", "expert"), None),
            P(("pipe", "expert"), None),
            P(("pipe", "expert"), None),
            P(("pipe", "expert"), None),
            P(("pipe", "expert"), None),
            P(("pipe", "expert"), None),
            P("pipe", None, None, "expert"),
            P("pipe", None, None, "expert"),
            P("pipe", "expert", None),
            P("pipe", "expert", None),
        ),
        out_specs=(
            P(("pipe", "expert"), None),
            P(("pipe", "expert"), None),
            P("pipe", "expert", None),
        ),
        check_vma=False,
    )
```
